256 devices in a mesh: dp: 8 (over y, core), ctx: 32 (over z, x).
Axes of the slice: x: 4, y: 4, z: 8, core: 2. Of those that a mesh axis runs over, the one named last changes fastest.
Arguments:
- hidden_in: bfloat16 [8, 4096, 5120], P('dp', 'ctx'), may hold values from -6 to 6
- value_weight: bfloat16 [5120, 512], replicated, may hold values from -0.078125 to 0.078125
- queries: bfloat16 [8, 4096, 2560], P('dp', 'ctx'), may hold values from -8 to 8
- keys: bfloat16 [8, 4096, 512], P('dp', 'ctx'), may hold values from -8 to 8
- out_grad: bfloat16 [8, 4096, 2560], P('dp', 'ctx'), may hold values from -6 to 6
Outputs:
- attended: bfloat16 [8, 4096, 2560], P('dp', 'ctx')
- query_grad: float32 [8, 4096, 2560], P('dp', 'ctx')
- key_grad: float32 [8, 4096, 512], P('dp', 'ctx')
- value_grad: float32 [8, 4096, 512], P('dp', 'ctx')
- weight_grad: float32 [5120, 512], P('ctx')
The draws below stay inside these ranges and needn't reach their ends.
All inputs are finite; a program needn't handle non-finite values.
Results may differ from the reference program's by a relative error of at most 0.028.
Values may be sent and summed in bfloat16 or wider, within the bound.
A program may use at most 192 MiB of HBM per device.

```python
import math
import jax
import jax.numpy as jnp
from jax import lax

D = 5120
HEADS_KV = 4
HEAD = 128
TOK_DEV = 128
GROUP = 5
Q_W = 2560
KV_W = 512
SEQ = 4096
REPLICAS = 8
N_CTX = 32


def draw_queries(key, part):
    key = jax.random.fold_in(key, 1)
    result_rows = jnp.clip(1.6 * jax.random.normal(key, (REPLICAS, SEQ, Q_W), jnp.float32), -8.0, 8.0)
    return result_rows.astype(jnp.bfloat16)


def draw_keys(key, part):
    key = jax.random.fold_in(key, 2)
    result_rows = jnp.clip(1.6 * jax.random.normal(key, (REPLICAS, SEQ, KV_W), jnp.float32), -8.0, 8.0)
    return result_rows.astype(jnp.bfloat16)


def with_spikes(entries, key, source, target, blocks, factor):
    def block_of(dim):
        return (jnp.arange(entries.shape[dim]) // (entries.shape[dim] // blocks)).reshape((-1,) + (1,) * (entries.ndim - 1 - dim))

    one_side = jax.random.permutation(key, blocks)[block_of(target)]
    other_side = (block_of(target) + blocks // 2) % blocks
    return jnp.where((block_of(source) == one_side) | (block_of(source) == other_side), factor * entries, entries)


def levels(key, dims, shards, low, top_value):
    factor_of = 1.0
    for axis_at, shards_of in shards:
        steps = jax.random.uniform(jax.random.fold_in(jax.random.fold_in(key, 6), axis_at), (shards_of,), jnp.float32, low / len(shards), top_value / len(shards))
        factor_of = factor_of * jnp.repeat(jnp.exp(steps), dims[axis_at] // shards_of).reshape((-1,) + (1,) * (len(dims) - 1 - axis_at))
    return factor_of


def noise(stream_key, shape, scale, most, cuts=(), kind=jnp.bfloat16):
    factor_of = levels(stream_key, shape, cuts, -0.22, 0.18) if cuts else 1.0
    array = jax.random.normal(stream_key, shape, jnp.float32) * scale * factor_of
    return jnp.minimum(jnp.maximum(array, -most), most).astype(kind)


def heavy_noise(key, dims, deviation, limit, split, heavy, kind=jnp.bfloat16):
    result = deviation * jax.random.normal(key, dims, jnp.float32)
    if split:
        result = result * levels(key, dims, split, -0.22, 0.18)
    return jnp.clip(with_spikes(result, jax.random.fold_in(key, 3), *heavy), -limit, limit).astype(kind)


def setup_inputs(seed: int = 0) -> dict:
    splits = jax.random.split(jax.random.key(seed), 6)
    return {
        "hidden_in": heavy_noise(splits[0], (REPLICAS, SEQ, D), 1.0, 6.0, ((0, 8), (1, 32)), (1, 2, 32, 2.75)),
        "value_weight": noise(splits[1], (D, KV_W), D ** -0.5, 0.078125),
        "queries": draw_queries(jax.random.fold_in(splits[5], 71), 0),
        "keys": draw_keys(jax.random.fold_in(splits[5], 71), 0),
        "out_grad": noise(splits[4], (REPLICAS, SEQ, Q_W), 1.0, 6.0, ((0, 8), (1, 32))),
    }


def head_pass(query_head, key_head, value_head, grad_head, allowed, score_scale):
    scores = jnp.dot(query_head, key_head.T, preferred_element_type=jnp.float32) * score_scale
    masked = jnp.where(allowed, scores, -jnp.inf)
    largest = lax.optimization_barrier(jnp.max(masked, axis=1, keepdims=True))
    log_total = largest + jnp.log(lax.optimization_barrier(jnp.sum(jnp.exp(masked - largest), axis=1, keepdims=True)))
    prob_full = jnp.exp(masked - log_total)
    weights = prob_full.astype(jnp.bfloat16)
    attended = jnp.dot(weights, value_head, preferred_element_type=jnp.float32).astype(jnp.bfloat16)
    row_delta = lax.optimization_barrier(jnp.sum(grad_head.astype(jnp.float32) * attended.astype(jnp.float32), axis=1, keepdims=True))
    prob_grad = jnp.dot(grad_head, value_head.T, preferred_element_type=jnp.float32)
    score_grad = (prob_full * (prob_grad - row_delta) * score_scale).astype(jnp.bfloat16)
    query_grad = jnp.dot(score_grad, key_head, preferred_element_type=jnp.float32)
    key_part = jnp.einsum('cij,cid->cjd', score_grad.reshape(N_CTX, TOK_DEV, SEQ).astype(jnp.float32), query_head.reshape(N_CTX, TOK_DEV, HEAD).astype(jnp.float32))
    value_part = jnp.einsum('cij,cid->cjd', weights.reshape(N_CTX, TOK_DEV, SEQ).astype(jnp.float32), grad_head.reshape(N_CTX, TOK_DEV, HEAD).astype(jnp.float32))
    return (attended, query_grad, key_part, value_part)

def group_pass(query_group, key_head, value_head, grad_group, allowed, score_scale):

    def head_step(part_sums, head_pair):
        attended, query_grad, key_part, value_part = head_pass(head_pair[0], key_head, value_head, head_pair[1], allowed, score_scale)
        return ((part_sums[0] + key_part, part_sums[1] + value_part), (attended, query_grad))
    zero_part = jnp.zeros((N_CTX, SEQ, HEAD), jnp.float32)
    (key_sum, value_sum), (attended, query_grad) = lax.scan(head_step, (zero_part, zero_part), (query_group, grad_group))
    key_round = lax.optimization_barrier(key_sum.astype(jnp.bfloat16)).astype(jnp.float32)
    value_round = lax.optimization_barrier(value_sum.astype(jnp.bfloat16)).astype(jnp.float32)
    key_grad = lax.optimization_barrier(jnp.sum(key_round, axis=0))
    value_grad = lax.optimization_barrier(jnp.sum(value_round, axis=0))
    return (attended, query_grad, key_grad, value_grad)

def replica_pass(query_rows, key_rows, value_rows, grad_rows, allowed, score_scale):
    query_groups = query_rows.reshape(SEQ, HEADS_KV, GROUP, HEAD).transpose(1, 2, 0, 3)
    grad_groups = grad_rows.reshape(SEQ, HEADS_KV, GROUP, HEAD).transpose(1, 2, 0, 3)
    key_groups = key_rows.reshape(SEQ, HEADS_KV, HEAD).transpose(1, 0, 2)
    value_groups = value_rows.reshape(SEQ, HEADS_KV, HEAD).transpose(1, 0, 2)

    def one_group(item):
        return group_pass(item[0], item[1], item[2], item[3], allowed, score_scale)
    attended, query_grad, key_grad, value_grad = lax.map(one_group, (query_groups, key_groups, value_groups, grad_groups))
    attended = attended.transpose(2, 0, 1, 3).reshape(SEQ, Q_W)
    query_grad = query_grad.transpose(2, 0, 1, 3).reshape(SEQ, Q_W)
    key_grad = key_grad.transpose(1, 0, 2).reshape(SEQ, KV_W)
    value_grad = value_grad.transpose(1, 0, 2).reshape(SEQ, KV_W)
    return (attended, query_grad, key_grad, value_grad)

def reference(hidden_in, value_weight, queries, keys, out_grad):
    score_scale = 1.0 / math.sqrt(HEAD)
    values = jnp.dot(hidden_in.reshape(REPLICAS * SEQ, D), value_weight, preferred_element_type=jnp.float32).astype(jnp.bfloat16).reshape(REPLICAS, SEQ, KV_W)
    position = jnp.arange(SEQ, dtype=jnp.int32)
    allowed = position[None, :] <= position[:, None]

    def one_replica(item):
        return replica_pass(item[0], item[1], item[2], item[3], allowed, score_scale)
    attended, query_grad, key_grad, value_grad = lax.map(one_replica, (queries, keys, values, out_grad))
    value_grad_round = value_grad.astype(jnp.bfloat16)
    hidden_blocks = hidden_in.reshape(REPLICAS * N_CTX, TOK_DEV, D)
    grad_blocks = value_grad_round.reshape(REPLICAS * N_CTX, TOK_DEV, KV_W)

    def add_term(grad_sum, block_pair):
        term = jnp.dot(block_pair[0].T, block_pair[1], preferred_element_type=jnp.float32)
        rounded = lax.optimization_barrier(term.astype(jnp.bfloat16)).astype(jnp.float32)
        return (grad_sum + rounded, None)
    grad_sum, _ = lax.scan(add_term, jnp.zeros((D, KV_W), jnp.float32), (hidden_blocks, grad_blocks))
    weight_grad = grad_sum / math.sqrt(REPLICAS * SEQ)
    return (attended, query_grad, key_grad, value_grad, weight_grad)
```

```python
import math

import jax
import jax.numpy as jnp
from jax import lax
from jax.experimental import pallas as pl
from jax.experimental.pallas import tpu as pltpu
from jax.sharding import PartitionSpec as P

BF = jnp.bfloat16
F32 = jnp.float32
SCALE = 1.0 / math.sqrt(128.0)
C2 = math.log2(math.e) * SCALE
NEG = -1e30
NX, NZ, NDP = 4, 8, 8
TOK = 128
BLK = NX * TOK
GROUP = 5
HEAD = 128
QG = GROUP * HEAD
WIDTH = 5120
ROWS = 160
PAD = 192
YROWS = PAD // 4
KCHUNKS = 4
UPS, DNS = 4, 3


def dot(a, b):
    return jnp.dot(a, b, preferred_element_type=F32)


def lanes(start, size):
    return pl.ds(pl.multiple_of(start, 128), size)


def rows(start, size):
    return pl.ds(pl.multiple_of(start, 16), size)


def kernel(
    hid_in, vw_in, q_in, k_in, do_in,
    att_out, dq_out, dk_out, dv_out, w_out,
    hid, vw, vals, qbuf, dobuf, kbuf, vbuf, ktbuf, qt, dot_t, pbuf, mhist, mrun, lrun, delta, ot, dqt,
    o_own, dq_own, dq_all, hid_t, hid_r,
    vs, vr, ks, kr, dv_own, dk_own, dv_all, dk_all,
    w_sib, w_sib_r, w_own, w_y, w_yr, w_z, w_zr, w_f, w_all,
    lsem, qsem, ksem, vsem, osem, hsem, asem, dqsem, gvsem, gksem, ksem_r, vsem_r, rvsem, rksem,
    csem, ysem, zsem, fsem,
):
    dp = lax.axis_index("dp")
    ctx = lax.axis_index("ctx")
    z, x = ctx // NX, ctx % NX
    y, c = dp // 2, dp % 2

    def at_x(d):
        return (dp, z * NX + (x + d) % NX)

    def at_z(d):
        return (dp, ((z + d) % NZ) * NX + x)

    def at_dp(d):
        return ((dp + d) % NDP, ctx)

    def remote(src, dst, sems, slot, device):
        return pltpu.make_async_remote_copy(
            src_ref=src, dst_ref=dst, send_sem=sems.at[0, slot], recv_sem=sems.at[1, slot],
            device_id=device, device_id_type=pl.DeviceIdType.MESH,
        )

    def wait_recv(dst, sems, slot):
        remote(dst, dst, sems, slot, at_x(1)).wait_recv()

    hid_copy = pltpu.make_async_copy(hid_in, hid, lsem.at[0])
    hid_copy.start()
    step_k = WIDTH // KCHUNKS
    vw_copies = []
    for i in range(KCHUNKS):
        part = pl.ds(i * step_k, step_k)
        vw_copies.append(pltpu.make_async_copy(vw_in.at[part], vw.at[part], lsem.at[1 + i]))
        vw_copies[-1].start()
    mine = rows(x * TOK, TOK)
    own_q = pltpu.make_async_copy(q_in.at[:, lanes(x * QG, QG)], qbuf.at[mine], lsem.at[5])
    own_k = pltpu.make_async_copy(k_in.at[:, lanes(x * HEAD, HEAD)], kbuf.at[z, mine], lsem.at[6])
    own_do = pltpu.make_async_copy(do_in.at[:, lanes(x * QG, QG)], dobuf.at[mine], lsem.at[7])
    own_q.start()
    own_k.start()
    own_do.start()

    barrier = pltpu.get_barrier_semaphore()
    partners = [at_x(d) for d in range(1, NX)] + [at_z(d) for d in range(1, NZ)]
    partners += [at_dp(d) for d in range(1, NDP)]
    for device in partners:
        pl.semaphore_signal(barrier, inc=1, device_id=device, device_id_type=pl.DeviceIdType.MESH)
    pl.semaphore_wait(barrier, len(partners))

    def exchange(source, target, sems):
        copies = []
        for d in range(1, NX):
            copies.append(remote(source((x + d) % NX), target(x), sems, d - 1, at_x(d)))
            copies[-1].start()
        return copies

    def arrive(target, sems):
        for d in range(1, NX):
            wait_recv(target((x + NX - d) % NX), sems, d - 1)

    sent = []
    to_k = lambda src: kbuf.at[z, rows(src * TOK, TOK)]
    to_v = lambda src: vbuf.at[z, rows(src * TOK, TOK)]
    to_q = lambda src: qbuf.at[rows(src * TOK, TOK)]
    to_do = lambda src: dobuf.at[rows(src * TOK, TOK)]
    to_hid = lambda src: hid_r.at[:, :, lanes(src * TOK, TOK)]
    sent += exchange(lambda dst: k_in.at[:, lanes(dst * HEAD, HEAD)], to_k, ksem)
    sent += exchange(lambda dst: q_in.at[:, lanes(dst * QG, QG)], to_q, qsem)

    hid_copy.wait()
    total = None
    for i in range(KCHUNKS):
        vw_copies[i].wait()
        part = slice(i * step_k, (i + 1) * step_k)
        term = dot(hid[:, part], vw[part, :])
        total = term if total is None else total + term
    vals[...] = total.astype(BF)
    vbuf[z, mine, :] = vals[:, lanes(x * HEAD, HEAD)]
    sent += exchange(lambda dst: vals.at[:, lanes(dst * HEAD, HEAD)], to_v, vsem)
    sent += exchange(lambda dst: do_in.at[:, lanes(dst * QG, QG)], to_do, osem)

    def ring(buf, sems, up, step):
        block = z - step + 1 if up else (z + step - 1) % NZ
        valid = (block >= 0) & (z < NZ - 1) if up else block < DNS
        slot = step - 1 if up else UPS + step - 1
        return block, valid, remote(
            buf.at[lax.rem(block + NZ, NZ)], buf.at[lax.rem(block + NZ, NZ)], sems, slot, at_z(1 if up else NZ - 1)
        )

    def ring_send(buf, sems, up, step):
        _, valid, copy = ring(buf, sems, up, step)
        pl.when(valid)(lambda: copy.start())

    def ring_sent(buf, sems, up, step):
        _, valid, copy = ring(buf, sems, up, step)
        pl.when(valid)(lambda: copy.wait_send())

    own_k.wait()
    arrive(to_k, ksem)
    ring_send(kbuf, ksem_r, True, 1)
    ring_send(kbuf, ksem_r, False, 1)
    for i in range(NZ):
        flipped = hid[:, i * 640:(i + 1) * 640].T
        for j in range(NX):
            hid_t[j, i] = flipped[j * ROWS:(j + 1) * ROWS]
    arrive(to_v, vsem)
    ring_send(vbuf, vsem_r, True, 1)
    ring_send(vbuf, vsem_r, False, 1)
    own_q.wait()
    arrive(to_q, qsem)
    sent += exchange(lambda dst: hid_t.at[dst], to_hid, hsem)
    own_hid = pltpu.make_async_copy(hid_t.at[x], to_hid(x), lsem.at[8])
    own_hid.start()

    for h in range(GROUP):
        qt[h] = qbuf[:, h * HEAD:(h + 1) * HEAD].T
    mrun[...] = jnp.full_like(mrun, NEG)
    lrun[...] = jnp.zeros_like(lrun)
    ot[...] = jnp.zeros_like(ot)
    dqt[...] = jnp.zeros_like(dqt)

    def forward(block, diagonal):
        k = kbuf[block]
        ktbuf[block] = k.T
        v_t = vbuf[block].T
        if diagonal:
            allowed = lax.broadcasted_iota(jnp.int32, (BLK, BLK), 0) <= lax.broadcasted_iota(
                jnp.int32, (BLK, BLK), 1
            )
        for h in range(GROUP):
            s = dot(k, qt[h])
            if diagonal:
                s = jnp.where(allowed, s, NEG)
            m_old = mrun[h]
            m_new = jnp.maximum(m_old, jnp.max(s, axis=0, keepdims=True))
            p = jnp.exp2((s - m_new) * C2)
            shrink = jnp.exp2((m_old - m_new) * C2)
            lrun[h] = lrun[h] * shrink + jnp.sum(p, axis=0, keepdims=True)
            p_round = p.astype(BF)
            pbuf[block * GROUP + h] = p_round
            mhist[block * GROUP + h] = m_new
            mrun[h] = m_new
            ot[h] = ot[h] * shrink + dot(v_t, p_round)

    forward(z, True)

    def forward_step(step, carry):
        up_block = z - step
        down_block = (z + step) % NZ
        up_valid = up_block >= 0
        down_valid = (down_block < DNS) & (step <= DNS)

        @pl.when(up_valid)
        def _():
            wait_recv(kbuf.at[up_block], ksem_r, step - 1)

            @pl.when((step < UPS) & (z < NZ - 1))
            def _():
                ring_send(kbuf, ksem_r, True, step + 1)

        @pl.when(down_valid)
        def _():
            wait_recv(kbuf.at[down_block], ksem_r, UPS + step - 1)

            @pl.when(step < DNS)
            def _():
                ring_send(kbuf, ksem_r, False, step + 1)

        @pl.when(up_valid)
        def _():
            wait_recv(vbuf.at[up_block], vsem_r, step - 1)

            @pl.when((step < UPS) & (z < NZ - 1))
            def _():
                ring_send(vbuf, vsem_r, True, step + 1)

        @pl.when(down_valid)
        def _():
            wait_recv(vbuf.at[down_block], vsem_r, UPS + step - 1)

            @pl.when(step < DNS)
            def _():
                ring_send(vbuf, vsem_r, False, step + 1)

        @pl.when(up_valid)
        def _():
            forward(up_block, False)

        @pl.when(down_valid & (down_block < z))
        def _():
            forward(down_block, False)

        return carry

    lax.fori_loop(1, UPS + 1, forward_step, 0)

    own_do.wait()
    arrive(to_do, osem)
    for h in range(GROUP):
        part = slice(h * HEAD, (h + 1) * HEAD)
        dot_t[h] = dobuf[:, part].T
        inverse = 1.0 / lrun[h]
        o = (ot[h] * inverse).astype(BF)
        o_own[:, part] = o.T
        delta[h] = jnp.sum(o.astype(F32) * dot_t[h].astype(F32), axis=0, keepdims=True)
        lrun[h] = inverse
    to_att = lambda src: att_out.at[:, lanes(src * QG, QG)]
    sent += exchange(lambda dst: o_own.at[rows(dst * TOK, TOK)], to_att, asem)
    own_att = pltpu.make_async_copy(o_own.at[mine], to_att(x), lsem.at[9])
    own_att.start()

    def grad_copy(send, recv, sems, slot, up):
        return remote(send.at[slot], recv.at[slot], sems, slot, at_z(1 if up else NZ - 1))

    def reduce_step(step, term, send, recv, sems):
        down_block = z - 5 + step
        up_block = (z + 4 - step) % NZ

        @pl.when(down_block >= 0)
        def _():
            own = term(down_block)
            slot = step - 1
            chained = (step >= 2) & (z < NZ - 1)

            @pl.when(chained)
            def _():
                wait_recv(recv.at[step - 2], sems, step - 2)
                send[slot] = (own + recv[step - 2].astype(F32)).astype(BF)

            @pl.when(jnp.logical_not(chained))
            def _():
                send[slot] = own.astype(BF)

            grad_copy(send, recv, sems, slot, False).start()

        up_valid = (step <= DNS) & (up_block < DNS)

        @pl.when(up_valid)
        def _():
            slot = UPS + step - 1

            @pl.when(step >= 2)
            def _():
                wait_recv(recv.at[slot - 1], sems, slot - 1)

            @pl.when(up_block < z)
            def _():
                own = term(up_block)

                @pl.when(step >= 2)
                def _():
                    send[slot] = (own + recv[slot - 1].astype(F32)).astype(BF)

                @pl.when(step < 2)
                def _():
                    send[slot] = own.astype(BF)

            @pl.when(up_block >= z)
            def _():
                send[slot] = recv[slot - 1]

            grad_copy(send, recv, sems, slot, True).start()

    def reduce_last(own, target, recv, sems):
        acc[...] = own

        @pl.when(z < NZ - 1)
        def _():
            wait_recv(recv.at[UPS - 1], sems, UPS - 1)
            acc[...] += recv[UPS - 1].astype(F32)

        @pl.when(z < DNS)
        def _():
            wait_recv(recv.at[UPS + DNS - 1], sems, UPS + DNS - 1)
            acc[...] += recv[UPS + DNS - 1].astype(F32)

        target[...] = acc[...].astype(BF)

    def reduce_sent(send, recv, sems):
        for step in range(1, UPS + 1):
            pl.when(z - 5 + step >= 0)(
                lambda: grad_copy(send, recv, sems, step - 1, False).wait_send()
            )
        for step in range(1, DNS + 1):
            pl.when((z + 4 - step) % NZ < DNS)(
                lambda: grad_copy(send, recv, sems, UPS + step - 1, True).wait_send()
            )

    acc = w_own.at[pl.ds(0, BLK), pl.ds(0, HEAD)]

    def value_term(block):
        total = None
        for h in range(GROUP):
            at = block * GROUP + h
            factor = jnp.exp2((mhist[at] - mrun[h]) * C2) * lrun[h]
            p = (pbuf[at].astype(F32) * factor).astype(BF)
            pbuf[at] = p
            term = dot(p, dobuf[:, h * HEAD:(h + 1) * HEAD])
            total = term if total is None else total + term
        return total

    def key_term(block):
        v = vbuf[block]
        k_t = ktbuf[block]
        total = None
        for h in range(GROUP):
            dp_t = dot(v, dot_t[h])
            ds = (pbuf[block * GROUP + h].astype(F32) * (dp_t - delta[h])).astype(BF)
            dqt[h] += dot(k_t, ds)
            term = dot(ds, qbuf[:, h * HEAD:(h + 1) * HEAD])
            total = term if total is None else total + term
        return total * SCALE

    def value_step(step, carry):
        reduce_step(step, value_term, vs, vr, rvsem)
        return carry

    lax.fori_loop(1, UPS + 1, value_step, 0)
    reduce_last(value_term(z), dv_own, vr, rvsem)
    to_dv = lambda src: dv_all.at[:, lanes(src * HEAD, HEAD)]
    sent += exchange(lambda dst: dv_own, to_dv, gvsem)
    dv_all[:, lanes(x * HEAD, HEAD)] = dv_own[...]

    far = lanes((1 - c) * 256, 256)
    near = lanes(c * 256, 256)
    sibling = (y * 2 + 1 - c, ctx)
    core_copy = remote(w_sib, w_sib_r, csem, 0, sibling)

    def stage_product():
        arrive(to_dv, gvsem)
        own_hid.wait()
        arrive(to_hid, hsem)
        dv_out[...] = dv_all[mine, :].astype(F32)

        def far_part(i, carry):
            at = rows(i * 320, 320)
            h2 = hid_r[pl.ds(i * 2, 2)].reshape(320, BLK)
            w_sib[at, :] = dot(h2, dv_all[:, far]).astype(BF)
            return carry

        def near_part(i, carry):
            at = rows(i * 320, 320)
            h2 = hid_r[pl.ds(i * 2, 2)].reshape(320, BLK)
            w_own[at, :] = dot(h2, dv_all[:, near])
            return carry

        lax.fori_loop(0, 4, far_part, 0)
        core_copy.start()
        lax.fori_loop(0, 4, near_part, 0)

    def y_copy(d):
        to = (y + d) % 4
        device = (to * 2 + c, ctx)
        return remote(w_y.at[:, rows(to * YROWS, YROWS)], w_yr.at[d - 1], ysem, d - 1, device)

    def stage_y():
        core_copy.wait_recv()
        for i in range(NZ):
            part = slice(i * ROWS, (i + 1) * ROWS)
            w_y[i, :ROWS] = (w_own[part, :] + w_sib_r[part, :].astype(F32)).astype(BF)
        w_y[:, ROWS:] = jnp.zeros((NZ, PAD - ROWS, 256), BF)
        for d in range(1, 4):
            y_copy(d).start()

    def z_copy(d):
        to = (z + d) % NZ
        return remote(w_z.at[to], w_zr.at[d - 1], zsem, d - 1, at_z(d))

    def stage_z():
        for d in range(1, 4):
            wait_recv(w_yr.at[d - 1], ysem, d - 1)
        total = w_y[:, rows(y * YROWS, YROWS), :].astype(F32)
        for d in range(1, 4):
            total += w_yr[d - 1].astype(F32)
        w_z[...] = total.astype(BF)
        for d in range(1, NZ):
            z_copy(d).start()

    def f_copy(d):
        return remote(w_f, w_all.at[c, rows(y * YROWS, YROWS)], fsem, d - 1, at_dp(d))

    def stage_f():
        for d in range(1, NZ):
            wait_recv(w_zr.at[d - 1], zsem, d - 1)
        total = w_z[z].astype(F32)
        for d in range(1, NZ):
            total += w_zr[d - 1].astype(F32)
        w_f[...] = (total * (1.0 / math.sqrt(32768.0))).astype(BF)
        w_all[c, rows(y * YROWS, YROWS), :] = w_f[...]
        for d in range(1, NDP):
            f_copy(d).start()

    def key_step(step, carry):
        reduce_step(step, key_term, ks, kr, rksem)
        pl.when(step == 1)(stage_product)
        pl.when(step == 2)(stage_y)
        pl.when(step == 3)(stage_z)
        pl.when(step == 4)(stage_f)
        return carry

    lax.fori_loop(1, UPS + 1, key_step, 0)
    last = key_term(z)
    for h in range(GROUP):
        dq_own[:, h * HEAD:(h + 1) * HEAD] = (dqt[h] * SCALE).astype(BF).T
    to_dq = lambda src: dq_all.at[:, lanes(src * QG, QG)]
    sent += exchange(lambda dst: dq_own.at[rows(dst * TOK, TOK)], to_dq, dqsem)
    dq_all[:, lanes(x * QG, QG)] = dq_own[mine, :]
    reduce_last(last, dk_own, kr, rksem)
    to_dk = lambda src: dk_all.at[:, lanes(src * HEAD, HEAD)]
    sent += exchange(lambda dst: dk_own.at[rows(dst * TOK, TOK)], to_dk, gksem)
    dk_all[:, lanes(x * HEAD, HEAD)] = dk_own[mine, :]

    for d in range(1, NDP):
        src = (dp + NDP - d) % NDP
        wait_recv(w_all.at[src % 2, rows(src // 2 * YROWS, YROWS)], fsem, d - 1)
    w_out[:, :256] = w_all[0, :ROWS].astype(F32)
    w_out[:, 256:] = w_all[1, :ROWS].astype(F32)
    arrive(to_dk, gksem)
    dk_out[...] = dk_all[...].astype(F32)
    arrive(to_dq, dqsem)
    dq_out[...] = dq_all[...].astype(F32)
    own_att.wait()
    arrive(to_att, asem)

    for copy in sent:
        copy.wait_send()
    for buf, sems in ((kbuf, ksem_r), (vbuf, vsem_r)):
        for step in range(1, UPS + 1):
            ring_sent(buf, sems, True, step)
        for step in range(1, DNS + 1):
            ring_sent(buf, sems, False, step)
    reduce_sent(vs, vr, rvsem)
    reduce_sent(ks, kr, rksem)
    core_copy.wait_send()
    for d in range(1, 4):
        y_copy(d).wait_send()
    for d in range(1, NZ):
        z_copy(d).wait_send()
    for d in range(1, NDP):
        f_copy(d).wait_send()


def per_device(hidden_in, value_weight, queries, keys, out_grad):
    vmem = pl.BlockSpec(memory_space=pltpu.VMEM)
    anywhere = pl.BlockSpec(memory_space=pl.ANY)
    dma = pltpu.SemaphoreType.DMA
    att, dq, dk, dv, w = pl.pallas_call(
        kernel,
        out_shape=[
            jax.ShapeDtypeStruct((TOK, 2560), BF),
            jax.ShapeDtypeStruct((TOK, 2560), F32),
            jax.ShapeDtypeStruct((TOK, 512), F32),
            jax.ShapeDtypeStruct((TOK, 512), F32),
            jax.ShapeDtypeStruct((ROWS, 512), F32),
        ],
        in_specs=[anywhere] * 5,
        out_specs=[anywhere, vmem, vmem, vmem, vmem],
        scratch_shapes=[
            pltpu.VMEM((TOK, WIDTH), BF),
            pltpu.VMEM((WIDTH, 512), BF),
            pltpu.VMEM((TOK, 512), BF),
            pltpu.VMEM((BLK, QG), BF),
            pltpu.VMEM((BLK, QG), BF),
            pltpu.VMEM((NZ, BLK, HEAD), BF),
            pltpu.VMEM((NZ, BLK, HEAD), BF),
            pltpu.VMEM((NZ, HEAD, BLK), BF),
            pltpu.VMEM((GROUP, HEAD, BLK), BF),
            pltpu.VMEM((GROUP, HEAD, BLK), BF),
            pltpu.VMEM((NZ * GROUP, BLK, BLK), BF),
            pltpu.VMEM((NZ * GROUP, 1, BLK), F32),
            pltpu.VMEM((GROUP, 1, BLK), F32),
            pltpu.VMEM((GROUP, 1, BLK), F32),
            pltpu.VMEM((GROUP, 1, BLK), F32),
            pltpu.VMEM((GROUP, HEAD, BLK), F32),
            pltpu.VMEM((GROUP, HEAD, BLK), F32),
            pltpu.VMEM((BLK, QG), BF),
            pltpu.VMEM((BLK, QG), BF),
            pltpu.VMEM((TOK, 2560), BF),
            pltpu.VMEM((NX, NZ, ROWS, TOK), BF),
            pltpu.VMEM((NZ, ROWS, BLK), BF),
            pltpu.VMEM((UPS + DNS, BLK, HEAD), BF),
            pltpu.VMEM((UPS + DNS, BLK, HEAD), BF),
            pltpu.VMEM((UPS + DNS, BLK, HEAD), BF),
            pltpu.VMEM((UPS + DNS, BLK, HEAD), BF),
            pltpu.VMEM((BLK, HEAD), BF),
            pltpu.VMEM((BLK, HEAD), BF),
            pltpu.VMEM((BLK, 512), BF),
            pltpu.VMEM((TOK, 512), BF),
            pltpu.VMEM((NZ * ROWS, 256), BF),
            pltpu.VMEM((NZ * ROWS, 256), BF),
            pltpu.VMEM((NZ * ROWS, 256), F32),
            pltpu.VMEM((NZ, PAD, 256), BF),
            pltpu.VMEM((3, NZ, YROWS, 256), BF),
            pltpu.VMEM((NZ, YROWS, 256), BF),
            pltpu.VMEM((NZ - 1, YROWS, 256), BF),
            pltpu.VMEM((YROWS, 256), BF),
            pltpu.VMEM((2, PAD, 256), BF),
            dma((10,)),
            dma((2, 3)),
            dma((2, 3)),
            dma((2, 3)),
            dma((2, 3)),
            dma((2, 3)),
            dma((2, 3)),
            dma((2, 3)),
            dma((2, 3)),
            dma((2, 3)),
            dma((2, UPS + DNS)),
            dma((2, UPS + DNS)),
            dma((2, UPS + DNS)),
            dma((2, UPS + DNS)),
            dma((2, 1)),
            dma((2, 3)),
            dma((2, NZ - 1)),
            dma((2, NDP - 1)),
        ],
        compiler_params=pltpu.CompilerParams(
            collective_id=0, has_side_effects=True, vmem_limit_bytes=60 * 2**20
        ),
    )(hidden_in[0], value_weight, queries[0], keys[0], out_grad[0])
    return (att[None], dq[None], dk[None], dv[None], w)


def solution(mesh):
    return jax.shard_map(
        per_device,
        mesh=mesh,
        in_specs=(
            P("dp", "ctx", None),
            P(),
            P("dp", "ctx", None),
            P("dp", "ctx", None),
            P("dp", "ctx", None),
        ),
        out_specs=(
            P("dp", "ctx", None),
            P("dp", "ctx", None),
            P("dp", "ctx", None),
            P("dp", "ctx", None),
            P("ctx", None),
        ),
        check_vma=False,
    )
```

```python
import math

import jax
import jax.numpy as jnp
from jax import lax
from jax.experimental import pallas as pl
from jax.experimental.pallas import tpu as pltpu
from jax.sharding import PartitionSpec as P

BF = jnp.bfloat16
F32 = jnp.float32
SCALE = 1.0 / math.sqrt(128.0)
C2 = math.log2(math.e) * SCALE
NEG = -1e30
NX, NZ, NDP = 4, 8, 8
TOK = 128
BLK = NX * TOK
GROUP = 5
HEAD = 128
QG = GROUP * HEAD
WIDTH = 5120
ROWS = 160
PAD = 192
YROWS = PAD // 4
KCHUNKS = 4
STEPS = 4
K_HOPS, V_HOPS = (4, 3), (3, 4)
KEY_HOPS = ((4, 3),)
VALUE_HOPS = ((4, 3), (3, 4), (4, 3), (3, 4))
Q_FIRST = 256


def dot(a, b):
    return jnp.dot(a, b, preferred_element_type=F32)


def lanes(start, size):
    return pl.ds(pl.multiple_of(start, 128), size)


def rows(start, size):
    return pl.ds(pl.multiple_of(start, 16), size)


def kernel(
    hid_in, vw_in, q_in, k_in, do_in,
    att_out, dq_out, dk_out, dv_out, w_all,
    hid, vw, vals, qbuf, dobuf, kbuf, vbuf, ktbuf, qt, dot_t, pbuf, mhist, mrun, lrun, delta, ot, dqt,
    o_own, dq_own, hid_t, hid_r, acc,
    vs, vr, ks, kr, dv_own, dk_own, dv_all,
    w_y, w_yr, w_z, w_zr, w_f,
    lsem, qsem, ksem, vsem, osem, hsem, asem, dqsem, gvsem, gosem, gksem, ksem_r, vsem_r, rvsem, rksem,
    csem, ysem, zsem, fsem,
):
    dp = lax.axis_index("dp")
    ctx = lax.axis_index("ctx")
    z, x = ctx // NX, ctx % NX
    y, c = dp // 2, dp % 2

    def at_x(d):
        return (dp, z * NX + (x + d) % NX)

    def at_z(d):
        return (dp, ((z + d) % NZ) * NX + x)

    def at_dp(d):
        return ((dp + d) % NDP, ctx)

    def remote(src, dst, sems, slot, device):
        return pltpu.make_async_remote_copy(
            src_ref=src, dst_ref=dst, send_sem=sems.at[0, slot], recv_sem=sems.at[1, slot],
            device_id=device, device_id_type=pl.DeviceIdType.MESH,
        )

    def wait_recv(dst, sems, slot):
        remote(dst, dst, sems, slot, at_x(1)).wait_recv()

    hid_copy = pltpu.make_async_copy(hid_in, hid, lsem.at[0])
    hid_copy.start()
    step_k = WIDTH // KCHUNKS
    vw_copies = []
    for i in range(KCHUNKS):
        part = pl.ds(i * step_k, step_k)
        vw_copies.append(pltpu.make_async_copy(vw_in.at[part], vw.at[part], lsem.at[1 + i]))
        vw_copies[-1].start()
    mine = rows(x * TOK, TOK)
    own_q = pltpu.make_async_copy(q_in.at[:, lanes(x * QG, QG)], qbuf.at[mine], lsem.at[5])
    own_k = pltpu.make_async_copy(k_in.at[:, lanes(x * HEAD, HEAD)], kbuf.at[z, mine], lsem.at[6])
    own_do = pltpu.make_async_copy(do_in.at[:, lanes(x * QG, QG)], dobuf.at[mine], lsem.at[7])
    own_q.start()
    own_k.start()
    own_do.start()

    barrier = pltpu.get_barrier_semaphore()
    partners = [at_x(d) for d in range(1, NX)] + [at_z(d) for d in range(1, NZ)]
    partners += [at_dp(d) for d in range(1, NDP)]
    partners += [(y * 2 + 1 - c, z * NX + (x + d) % NX) for d in range(1, NX)]
    for device in partners:
        pl.semaphore_signal(barrier, inc=1, device_id=device, device_id_type=pl.DeviceIdType.MESH)
    pl.semaphore_wait(barrier, len(partners))

    def exchange(source, target, sems, first=0):
        copies = []
        for d in range(1, NX):
            copies.append(remote(source((x + d) % NX), target(x), sems, first + d - 1, at_x(d)))
            copies[-1].start()
        return copies

    def arrive(target, sems, first=0):
        for d in range(1, NX):
            wait_recv(target((x + NX - d) % NX), sems, first + d - 1)

    sent = []
    to_k = lambda src: kbuf.at[z, rows(src * TOK, TOK)]
    to_v = lambda src: vbuf.at[z, rows(src * TOK, TOK)]
    to_q = lambda src: qbuf.at[rows(src * TOK, TOK), pl.ds(0, Q_FIRST)]
    to_q2 = lambda src: qbuf.at[rows(src * TOK, TOK), pl.ds(Q_FIRST, QG - Q_FIRST)]
    to_do = lambda src: dobuf.at[rows(src * TOK, TOK)]
    to_hid = lambda src: hid_r.at[:, :, lanes(c * BLK + src * TOK, TOK)]
    sent += exchange(lambda dst: k_in.at[:, lanes(dst * HEAD, HEAD)], to_k, ksem)
    sent += exchange(lambda dst: q_in.at[:, lanes(dst * QG, Q_FIRST)], to_q, qsem)

    def ring_send(buf, sems, hops, up, step, act=lambda copy: copy.start()):
        block = z - step + 1 if up else (z + step - 1) % NZ
        valid = (block >= 0) & (z < NZ - 1) if up else block < hops[1]
        slot = step - 1 if up else hops[0] + step - 1
        at = buf.at[(block + NZ) % NZ]
        pl.when(valid)(lambda: act(remote(at, at, sems, slot, at_z(1 if up else NZ - 1))))

    def ring_first(buf, sems, hops):
        ring_send(buf, sems, hops, True, 1)
        ring_send(buf, sems, hops, False, 1)

    hid_copy.wait()
    for i in range(NZ):
        flipped = hid[:, i * 640:(i + 1) * 640].T
        for j in range(NX):
            hid_t[j, i] = flipped[j * ROWS:(j + 1) * ROWS]
    for copy in vw_copies:
        copy.wait()
    vals[...] = dot(hid[...], vw[...]).astype(BF)
    vbuf[z, mine, :] = vals[:, lanes(x * HEAD, HEAD)]
    sent += exchange(lambda dst: vals.at[:, lanes(dst * HEAD, HEAD)], to_v, vsem)
    sent += exchange(
        lambda dst: q_in.at[:, lanes(dst * QG + Q_FIRST, QG - Q_FIRST)], to_q2, qsem, 3
    )
    own_k.wait()
    arrive(to_k, ksem)
    ring_first(kbuf, ksem_r, K_HOPS)
    arrive(to_v, vsem)
    ring_first(vbuf, vsem_r, V_HOPS)
    sent += exchange(lambda dst: do_in.at[:, lanes(dst * QG, QG)], to_do, osem)
    own_q.wait()
    arrive(to_q, qsem)
    arrive(to_q2, qsem, 3)
    sent += exchange(lambda dst: hid_t.at[dst], to_hid, hsem)
    own_hid = pltpu.make_async_copy(hid_t.at[x], to_hid(x), lsem.at[8])
    own_hid.start()

    for h in range(GROUP):
        qt[h] = qbuf[:, h * HEAD:(h + 1) * HEAD].T
    mrun[...] = jnp.full_like(mrun, NEG)
    lrun[...] = jnp.zeros_like(lrun)
    ot[...] = jnp.zeros_like(ot)
    dqt[...] = jnp.zeros_like(dqt)

    def forward(block, diagonal):
        k = kbuf[block]
        ktbuf[block] = k.T
        v_t = jnp.concatenate([vbuf[block].T, jnp.ones((16, BLK), BF)], axis=0)
        if diagonal:
            allowed = lax.broadcasted_iota(jnp.int32, (BLK, BLK), 0) <= lax.broadcasted_iota(
                jnp.int32, (BLK, BLK), 1
            )

        def weigh(h, s):
            if diagonal:
                s = jnp.where(allowed, s, NEG)
            m_old = mrun[h]
            m_new = jnp.maximum(m_old, jnp.max(s, axis=0, keepdims=True))
            shift = m_new * C2
            p = jnp.exp2(s * C2 - shift).astype(BF)
            pbuf[block * GROUP + h] = p
            mhist[block * GROUP + h] = m_new
            mrun[h] = m_new
            return p, jnp.exp2(m_old * C2 - shift)

        def gather(h, p, shrink):
            o = dot(v_t, p)
            ot[h] = ot[h] * shrink + o[:HEAD]
            lrun[h] = lrun[h] * shrink + o[HEAD:HEAD + 1]

        s = dot(k, qt[0])
        held = None
        for h in range(GROUP):
            s_next = dot(k, qt[h + 1]) if h + 1 < GROUP else None
            if held is not None:
                gather(*held)
            held = (h, *weigh(h, s))
            s = s_next
        gather(*held)

    def pass_on(buf, sems, hops, step):
        ups, dns = hops

        @pl.when((z - step >= 0) & (step <= ups))
        def _():
            wait_recv(buf.at[(z - step + NZ) % NZ], sems, step - 1)
            pl.when(step < ups)(lambda: ring_send(buf, sems, hops, True, step + 1))

        @pl.when(((z + step) % NZ < dns) & (step <= dns))
        def _():
            wait_recv(buf.at[(z + step) % NZ], sems, ups + step - 1)
            pl.when(step < dns)(lambda: ring_send(buf, sems, hops, False, step + 1))

    pass_on(kbuf, ksem_r, K_HOPS, 1)
    forward(z, True)
    pass_on(vbuf, vsem_r, V_HOPS, 1)

    def forward_step(step, carry):
        below = (z + step) % NZ
        pl.when(z - step >= 0)(lambda: forward((z - step + NZ) % NZ, False))
        pass_on(kbuf, ksem_r, K_HOPS, step + 1)
        pl.when((step < STEPS) & (below < NZ - 1 - STEPS) & (below < z))(lambda: forward(below, False))
        pass_on(vbuf, vsem_r, V_HOPS, step + 1)
        return carry

    lax.fori_loop(1, STEPS + 1, forward_step, 0)

    own_do.wait()
    arrive(to_do, osem)
    for h in range(GROUP):
        part = slice(h * HEAD, (h + 1) * HEAD)
        dot_t[h] = dobuf[:, part].T
        inverse = 1.0 / lrun[h]
        o = (ot[h] * inverse).astype(BF)
        o_own[:, part] = o.T
        delta[h] = jnp.sum(o.astype(F32) * dot_t[h].astype(F32), axis=0, keepdims=True)
        lrun[h] = inverse
    to_att = lambda src: att_out.at[:, lanes(src * QG, QG)]
    sent += exchange(lambda dst: o_own.at[rows(dst * TOK, TOK)], to_att, asem)
    own_att = pltpu.make_async_copy(o_own.at[mine], to_att(x), lsem.at[9])
    own_att.start()

    def hop_copy(send, recv, sems, up, slot, part, parts):
        at = pl.ds(part * (BLK // parts), BLK // parts)
        return remote(
            send.at[slot, at], recv.at[slot, at], sems, part * (NZ - 1) + slot, at_z(1 if up else NZ - 1)
        )

    def hop_plan(hops, step, up):
        ups = hops[1]
        if up:
            block = (z + ups + 1 - step) % NZ
            return block, (step <= ups) & (block < ups), hops[0] + step - 1
        block = z - hops[0] - 1 + step
        return (block + NZ) % NZ, (step <= hops[0]) & (block >= 0), step - 1

    def reduce_step(step, term, send, recv, sems, plan):
        parts = len(plan)
        size = BLK // parts
        for part in range(parts):
            at = pl.ds(part * size, size)
            for up in (False, True):
                block, valid, slot = hop_plan(plan[part], step, up)

                @pl.when(valid)
                def _():
                    if up:

                        @pl.when(block < z)
                        def _():
                            acc[:size] = term(block, part, parts)

                        @pl.when(block >= z)
                        def _():
                            acc[:size] = jnp.zeros((size, HEAD), F32)
                    else:
                        acc[:size] = term(block, part, parts)

                    @pl.when((step >= 2) if up else (step >= 2) & (z < NZ - 1))
                    def _():
                        wait_recv(recv.at[slot - 1, at], sems, part * (NZ - 1) + slot - 1)
                        acc[:size] += recv[slot - 1, at].astype(F32)

                    send[slot, at] = acc[:size].astype(BF)
                    hop_copy(send, recv, sems, up, slot, part, parts).start()

    def reduce_last(term, target, recv, sems, plan, done=lambda part, at: None):
        parts = len(plan)
        size = BLK // parts
        for part, (dns, ups) in enumerate(plan):
            at = pl.ds(part * size, size)
            acc[:size] = term(z, part, parts)
            for valid, slot in ((z < NZ - 1, dns - 1), (z < ups, dns + ups - 1)):

                @pl.when(valid)
                def _():
                    wait_recv(recv.at[slot, at], sems, part * (NZ - 1) + slot)
                    acc[:size] += recv[slot, at].astype(F32)

            target[at] = acc[:size].astype(BF)
            done(part, at)

    def reduce_sent(send, recv, sems, plan):
        for part in range(len(plan)):
            for up in (False, True):
                for step in range(1, STEPS + 1):
                    if step <= plan[part][1 if up else 0]:
                        _, valid, slot = hop_plan(plan[part], step, up)
                        pl.when(valid)(
                            lambda: hop_copy(send, recv, sems, up, slot, part, len(plan)).wait_send()
                        )

    def value_term(block, part=0, parts=1):
        keys = pl.ds(part * (BLK // parts), BLK // parts)
        total = None
        for h in range(GROUP):
            at = block * GROUP + h
            factor = jnp.exp2((mhist[at] - mrun[h]) * C2) * lrun[h]
            p = (pbuf[at, keys].astype(F32) * factor).astype(BF)
            pbuf[at, keys] = p
            term = dot(p, dobuf[:, h * HEAD:(h + 1) * HEAD])
            total = term if total is None else total + term
        return total

    def key_term(block, part=0, parts=1):
        v = vbuf[block]
        k_t = ktbuf[block]
        total = None
        dp_next = dot(v, dot_t[0])
        for h in range(GROUP):
            dp_t = dp_next
            dp_next = dot(v, dot_t[h + 1]) if h + 1 < GROUP else None
            ds = (pbuf[block * GROUP + h].astype(F32) * (dp_t - delta[h])).astype(BF)
            dqt[h] += dot(k_t, ds)
            term = dot(ds, qbuf[:, h * HEAD:(h + 1) * HEAD])
            total = term if total is None else total + term
        return total * SCALE

    def value_step(step, carry):
        reduce_step(step, value_term, vs, vr, rvsem, VALUE_HOPS)
        return carry

    lax.fori_loop(1, STEPS + 1, value_step, 0)
    own_hid.wait()
    arrive(to_hid, hsem)
    sibling = (y * 2 + 1 - c, ctx)
    hid_half = hid_r.at[:, :, lanes(c * BLK, BLK)]
    hid_copy2 = remote(hid_half, hid_half, csem, 0, sibling)
    hid_copy2.start()

    def share(part, d):
        at = pl.ds(part * (BLK // len(VALUE_HOPS)), BLK // len(VALUE_HOPS))
        slot = (part * 2 + x % 2) * 2 + c
        return pltpu.make_async_remote_copy(
            src_ref=dv_own.at[at],
            dst_ref=dv_all.at[c, at, lanes(x % 2 * HEAD, HEAD)],
            send_sem=gvsem.at[0, part * NX + d],
            recv_sem=gvsem.at[1, slot],
            device_id=(y * 2 + x // 2, z * NX + (x + d) % NX),
            device_id_type=pl.DeviceIdType.MESH,
        )

    def share_all(part, at):
        for d in range(1, NX):
            share(part, d).start()
        pl.when(x // 2 != c)(lambda: share(part, 0).start())

        @pl.when(x // 2 == c)
        def _():
            dv_all[c, at, lanes(x % 2 * HEAD, HEAD)] = dv_own[at]

    reduce_last(value_term, dv_own, vr, rvsem, VALUE_HOPS, share_all)
    to_dv = lambda src: dv_out.at[:, lanes(src * HEAD, HEAD)]
    sent += exchange(lambda dst: dv_own.at[rows(dst * TOK, TOK)], to_dv, gosem)
    dv_out[:, lanes(x * HEAD, HEAD)] = dv_own[mine, :]

    halves = (0, 1)

    def y_copy(i, d):
        to = (y + d) % 4
        return remote(
            w_y.at[i, :, rows(to * YROWS, YROWS)], w_yr.at[i, d - 1], ysem, i * 3 + d - 1, (to * 2 + c, ctx)
        )

    def stage_product():
        hid_copy2.wait_recv()
        for part in range(len(VALUE_HOPS)):
            at = pl.ds(part * (BLK // len(VALUE_HOPS)), BLK // len(VALUE_HOPS))
            for j in (0, 1):
                for core in (0, 1):

                    @pl.when((x != c * 2 + j) | (c != core))
                    def _():
                        wait_recv(dv_all.at[core, at, pl.ds(j * HEAD, HEAD)], gvsem, (part * 2 + j) * 2 + core)

        w_y[:, :, ROWS:] = jnp.zeros((2, NZ, PAD - ROWS, HEAD), BF)
        h_rows = hid_r[...].reshape(NZ * ROWS, 2 * BLK)
        total = dot(h_rows, dv_all[...].reshape(2 * BLK, 256)).astype(BF)
        for i in halves:
            w_y[i, :, :ROWS] = total[:, i * HEAD:(i + 1) * HEAD].reshape(NZ, ROWS, HEAD)
            for d in range(1, 4):
                y_copy(i, d).start()

    def z_copy(i, d):
        return remote(w_z.at[i, (z + d) % NZ], w_zr.at[i, d - 1], zsem, i * (NZ - 1) + d - 1, at_z(d))

    def stage_z():
        for i in halves:
            total = w_y[i, :, rows(y * YROWS, YROWS), :].astype(F32)
            for d in range(1, 4):
                wait_recv(w_yr.at[i, d - 1], ysem, i * 3 + d - 1)
                total += w_yr[i, d - 1].astype(F32)
            w_z[i] = total.astype(BF)
            for d in range(1, NZ):
                z_copy(i, d).start()

    def f_copy(i, d):
        target = w_all.at[c * 2 + i, rows(y * YROWS, YROWS)]
        return remote(w_f.at[i], target, fsem, i * (NDP - 1) + d - 1, at_dp(d))

    def stage_f():
        for i in halves:
            total = w_z[i, z].astype(F32)
            for d in range(1, NZ):
                wait_recv(w_zr.at[i, d - 1], zsem, i * (NZ - 1) + d - 1)
                total += w_zr[i, d - 1].astype(F32)
            w_f[i] = (total * (1.0 / math.sqrt(32768.0))).astype(BF)
            w_all[c * 2 + i, rows(y * YROWS, YROWS), :] = w_f[i]
            for d in range(1, NDP):
                f_copy(i, d).start()

    def key_step(step, carry):
        reduce_step(step, key_term, ks, kr, rksem, KEY_HOPS)
        pl.when(step == 1)(stage_product)
        return carry

    lax.fori_loop(1, STEPS + 1, key_step, 0)
    last = key_term(z)
    for h in range(GROUP):
        dq_own[:, h * HEAD:(h + 1) * HEAD] = (dqt[h] * SCALE).astype(BF).T
    to_dq = lambda src: dq_out.at[:, lanes(src * QG, QG)]
    sent += exchange(lambda dst: dq_own.at[rows(dst * TOK, TOK)], to_dq, dqsem)
    own_dq = pltpu.make_async_copy(dq_own.at[mine], to_dq(x), lsem.at[0])
    own_dq.start()
    stage_z()
    reduce_last(lambda block, part, parts: last, dk_own, kr, rksem, KEY_HOPS)
    to_dk = lambda src: dk_out.at[:, lanes(src * HEAD, HEAD)]
    sent += exchange(lambda dst: dk_own.at[rows(dst * TOK, TOK)], to_dk, gksem)
    dk_out[:, lanes(x * HEAD, HEAD)] = dk_own[mine, :]
    stage_f()

    own_dq.wait()
    own_att.wait()
    arrive(to_att, asem)
    for copy in sent:
        copy.wait_send()
    for buf, sems, hops in ((kbuf, ksem_r, K_HOPS), (vbuf, vsem_r, V_HOPS)):
        for up in (True, False):
            for step in range(1, hops[0 if up else 1] + 1):
                ring_send(buf, sems, hops, up, step, lambda copy: copy.wait_send())
    reduce_sent(vs, vr, rvsem, VALUE_HOPS)
    reduce_sent(ks, kr, rksem, KEY_HOPS)
    for i in halves:
        for d in range(1, 4):
            y_copy(i, d).wait_send()
        for d in range(1, NZ):
            z_copy(i, d).wait_send()
    hid_copy2.wait_send()
    for part in range(len(VALUE_HOPS)):
        for d in range(1, NX):
            share(part, d).wait_send()
        pl.when(x // 2 != c)(lambda: share(part, 0).wait_send())
    arrive(to_dv, gosem)
    arrive(to_dk, gksem)
    arrive(to_dq, dqsem)
    for i in halves:
        for d in range(1, NDP):
            src = (dp + NDP - d) % NDP
            target = w_all.at[src % 2 * 2 + i, rows(src // 2 * YROWS, YROWS)]
            wait_recv(target, fsem, i * (NDP - 1) + d - 1)
            f_copy(i, d).wait_send()


def finish(att, dq, dk, dv, w, att_out, dq_out, dk_out, dv_out, w_out):
    att_out[...] = att[...]
    dq_out[...] = dq[...].astype(F32)
    dk_out[...] = dk[...].astype(F32)
    dv_out[...] = dv[...].astype(F32)
    for i in range(4):
        w_out[:, i * HEAD:(i + 1) * HEAD] = w[i, :ROWS].astype(F32)


def per_device(hidden_in, value_weight, queries, keys, out_grad):
    vmem = pl.BlockSpec(memory_space=pltpu.VMEM)
    anywhere = pl.BlockSpec(memory_space=pl.ANY)
    dma = pltpu.SemaphoreType.DMA
    parts = pl.pallas_call(
        kernel,
        out_shape=[
            jax.ShapeDtypeStruct((TOK, 2560), BF),
            jax.ShapeDtypeStruct((TOK, 2560), BF),
            jax.ShapeDtypeStruct((TOK, 512), BF),
            jax.ShapeDtypeStruct((TOK, 512), BF),
            jax.ShapeDtypeStruct((4, PAD, HEAD), BF),
        ],
        in_specs=[anywhere] * 5,
        out_specs=[anywhere, anywhere, vmem, vmem, vmem],
        scratch_shapes=[
            pltpu.VMEM((TOK, WIDTH), BF),
            pltpu.VMEM((WIDTH, 512), BF),
            pltpu.VMEM((TOK, 512), BF),
            pltpu.VMEM((BLK, QG), BF),
            pltpu.VMEM((BLK, QG), BF),
            pltpu.VMEM((NZ, BLK, HEAD), BF),
            pltpu.VMEM((NZ, BLK, HEAD), BF),
            pltpu.VMEM((NZ, HEAD, BLK), BF),
            pltpu.VMEM((GROUP, HEAD, BLK), BF),
            pltpu.VMEM((GROUP, HEAD, BLK), BF),
            pltpu.VMEM((NZ * GROUP, BLK, BLK), BF),
            pltpu.VMEM((NZ * GROUP, 1, BLK), F32),
            pltpu.VMEM((GROUP, 1, BLK), F32),
            pltpu.VMEM((GROUP, 1, BLK), F32),
            pltpu.VMEM((GROUP, 1, BLK), F32),
            pltpu.VMEM((GROUP, HEAD, BLK), F32),
            pltpu.VMEM((GROUP, HEAD, BLK), F32),
            pltpu.VMEM((BLK, QG), BF),
            pltpu.VMEM((BLK, QG), BF),
            pltpu.VMEM((NX, NZ, ROWS, TOK), BF),
            pltpu.VMEM((NZ, ROWS, 2 * BLK), BF),
            pltpu.VMEM((BLK, HEAD), F32),
            pltpu.VMEM((NZ - 1, BLK, HEAD), BF),
            pltpu.VMEM((NZ - 1, BLK, HEAD), BF),
            pltpu.VMEM((NZ - 1, BLK, HEAD), BF),
            pltpu.VMEM((NZ - 1, BLK, HEAD), BF),
            pltpu.VMEM((BLK, HEAD), BF),
            pltpu.VMEM((BLK, HEAD), BF),
            pltpu.VMEM((2, BLK, 256), BF),
            pltpu.VMEM((2, NZ, PAD, HEAD), BF),
            pltpu.VMEM((2, 3, NZ, YROWS, HEAD), BF),
            pltpu.VMEM((2, NZ, YROWS, HEAD), BF),
            pltpu.VMEM((2, NZ - 1, YROWS, HEAD), BF),
            pltpu.VMEM((2, YROWS, HEAD), BF),
            dma((10,)),
            dma((2, 6)),
            dma((2, 3)),
            dma((2, 3)),
            dma((2, 3)),
            dma((2, 3)),
            dma((2, 3)),
            dma((2, 3)),
            dma((2, 16)),
            dma((2, 3)),
            dma((2, 3)),
            dma((2, NZ - 1)),
            dma((2, NZ - 1)),
            dma((2, 4 * (NZ - 1))),
            dma((2, NZ - 1)),
            dma((2, 1)),
            dma((2, 6)),
            dma((2, 2 * (NZ - 1))),
            dma((2, 2 * (NDP - 1))),
        ],
        compiler_params=pltpu.CompilerParams(
            collective_id=0, has_side_effects=True, vmem_limit_bytes=60 * 2**20
        ),
    )(hidden_in[0], value_weight, queries[0], keys[0], out_grad[0])
    att, dq, dk, dv, w = pl.pallas_call(
        finish,
        out_shape=[
            jax.ShapeDtypeStruct((TOK, 2560), BF),
            jax.ShapeDtypeStruct((TOK, 2560), F32),
            jax.ShapeDtypeStruct((TOK, 512), F32),
            jax.ShapeDtypeStruct((TOK, 512), F32),
            jax.ShapeDtypeStruct((ROWS, 512), F32),
        ],
        in_specs=[vmem] * 5,
        out_specs=[vmem] * 5,
    )(*parts)
    return (att[None], dq[None], dk[None], dv[None], w)


def solution(mesh):
    return jax.shard_map(
        per_device,
        mesh=mesh,
        in_specs=(
            P("dp", "ctx", None),
            P(),
            P("dp", "ctx", None),
            P("dp", "ctx", None),
            P("dp", "ctx", None),
        ),
        out_specs=(
            P("dp", "ctx", None),
            P("dp", "ctx", None),
            P("dp", "ctx", None),
            P("dp", "ctx", None),
            P("ctx", None),
        ),
        check_vma=False,
    )
```

```python
import math

import jax
import jax.numpy as jnp
from jax import lax
from jax.experimental import pallas as pl
from jax.experimental.pallas import tpu as pltpu
from jax.sharding import PartitionSpec as P

BF = jnp.bfloat16
F32 = jnp.float32
SCALE = 1.0 / math.sqrt(128.0)
C2 = math.log2(math.e) * SCALE
NEG = -1e30
NX, NZ, NDP = 4, 8, 8
TOK = 128
BLK = NX * TOK
GROUP = 5
HEAD = 128
QG = GROUP * HEAD
WIDTH = 5120
ROWS = 160
YROWS, YLESS = 48, 32
KCHUNKS = 4
STEPS = 4
K_HOPS, V_HOPS = (4, 3, 1), (3, 4, 2)
KEY_HOPS = ((4, 3), (3, 4))
VALUE_HOPS = ((4, 3), (3, 4), (4, 3), (3, 4))
Q_FIRST = 256


def dot(a, b):
    return jnp.dot(a, b, preferred_element_type=F32)


def lanes(start, size):
    return pl.ds(pl.multiple_of(start, 128), size)


def rows(start, size):
    return pl.ds(pl.multiple_of(start, 16), size)


def kernel(
    hid_in, vw_in, q_in, k_in, do_in,
    att_out, dq_out, dk_out, dv_out, w_all,
    hid, vw, vals, qbuf, dobuf, kbuf, vbuf, ktbuf, qt, dot_t, pbuf, mhist, mrun, lrun, delta, ot, dqt,
    o_own, dq_own, hid_t, hid_r, acc,
    vs, vr, ks, kr, dv_own, dk_own, dv_all,
    w_y, w_yr, w_z, w_zr, w_f,
    lsem, qsem, ksem, vsem, osem, hsem, asem, dqsem, gvsem, gosem, gksem, ksem_r, vsem_r, rvsem, rksem,
    csem, ysem, zsem, fsem,
):
    dp = lax.axis_index("dp")
    ctx = lax.axis_index("ctx")
    z, x = ctx // NX, ctx % NX
    y, c = dp // 2, dp % 2

    def at_x(d):
        return (dp, z * NX + (x + d) % NX)

    def at_z(d):
        return (dp, ((z + d) % NZ) * NX + x)

    def at_dp(d):
        return ((dp + d) % NDP, ctx)

    def remote(src, dst, sems, slot, device):
        return pltpu.make_async_remote_copy(
            src_ref=src, dst_ref=dst, send_sem=sems.at[0, slot], recv_sem=sems.at[1, slot],
            device_id=device, device_id_type=pl.DeviceIdType.MESH,
        )

    def wait_recv(dst, sems, slot):
        remote(dst, dst, sems, slot, at_x(1)).wait_recv()

    hid_copy = pltpu.make_async_copy(hid_in, hid, lsem.at[0])
    hid_copy.start()
    step_k = WIDTH // KCHUNKS
    vw_copies = []
    for i in range(KCHUNKS):
        part = pl.ds(i * step_k, step_k)
        vw_copies.append(pltpu.make_async_copy(vw_in.at[part], vw.at[part], lsem.at[1 + i]))
        vw_copies[-1].start()
    mine = rows(x * TOK, TOK)
    own_q = pltpu.make_async_copy(q_in.at[:, lanes(x * QG, QG)], qbuf.at[mine], lsem.at[5])
    own_k = pltpu.make_async_copy(k_in.at[:, lanes(x * HEAD, HEAD)], kbuf.at[z, mine], lsem.at[6])
    own_do = pltpu.make_async_copy(do_in.at[:, lanes(x * QG, QG)], dobuf.at[mine], lsem.at[7])
    own_q.start()
    own_k.start()
    own_do.start()

    barrier = pltpu.get_barrier_semaphore()
    partners = [at_x(d) for d in range(1, NX)] + [at_z(d) for d in range(1, NZ)]
    partners += [at_dp(d) for d in range(1, NDP)]
    partners += [(y * 2 + 1 - c, z * NX + (x + d) % NX) for d in range(1, NX)]
    for device in partners:
        pl.semaphore_signal(barrier, inc=1, device_id=device, device_id_type=pl.DeviceIdType.MESH)
    pl.semaphore_wait(barrier, len(partners))

    def exchange(source, target, sems, first=0):
        copies = []
        for d in range(1, NX):
            copies.append(remote(source((x + d) % NX), target(x), sems, first + d - 1, at_x(d)))
            copies[-1].start()
        return copies

    def arrive(target, sems, first=0):
        for d in range(1, NX):
            wait_recv(target((x + NX - d) % NX), sems, first + d - 1)

    sent = []
    to_k = lambda src: kbuf.at[z, rows(src * TOK, TOK)]
    to_v = lambda src: vbuf.at[z, rows(src * TOK, TOK)]
    to_q = lambda src: qbuf.at[rows(src * TOK, TOK), pl.ds(0, Q_FIRST)]
    to_q2 = lambda src: qbuf.at[rows(src * TOK, TOK), pl.ds(Q_FIRST, QG - Q_FIRST)]
    to_do = lambda src: dobuf.at[rows(src * TOK, TOK)]
    to_hid = lambda src: hid_r.at[:, :, lanes(c * BLK + src * TOK, TOK)]
    sent += exchange(lambda dst: k_in.at[:, lanes(dst * HEAD, HEAD)], to_k, ksem)
    sent += exchange(lambda dst: q_in.at[:, lanes(dst * QG, Q_FIRST)], to_q, qsem)

    def ring_at(buf, block, part, parts):
        return buf.at[(block + NZ) % NZ, pl.ds(part * (BLK // parts), BLK // parts)]

    def ring_send(buf, sems, hops, up, step, part, act=lambda copy: copy.start()):
        ups, dns, parts = hops
        block = z - step + 1 if up else (z + step - 1) % NZ
        valid = (block >= 0) & (z < NZ - 1) if up else block < dns
        slot = part * (NZ - 1) + (step - 1 if up else ups + step - 1)
        at = ring_at(buf, block, part, parts)
        pl.when(valid)(lambda: act(remote(at, at, sems, slot, at_z(1 if up else NZ - 1))))

    def ring_first(buf, sems, hops):
        for part in range(hops[2]):
            ring_send(buf, sems, hops, True, 1, part)
            ring_send(buf, sems, hops, False, 1, part)

    hid_copy.wait()
    for copy in vw_copies:
        copy.wait()
    vals[...] = dot(hid[...], vw[...]).astype(BF)
    vbuf[z, mine, :] = vals[:, lanes(x * HEAD, HEAD)]
    sent += exchange(lambda dst: vals.at[:, lanes(dst * HEAD, HEAD)], to_v, vsem)
    sent += exchange(
        lambda dst: q_in.at[:, lanes(dst * QG + Q_FIRST, QG - Q_FIRST)], to_q2, qsem, 3
    )
    for i in range(NZ):
        flipped = hid[:, i * 640:(i + 1) * 640].T
        for j in range(NX):
            hid_t[j, i] = flipped[j * ROWS:(j + 1) * ROWS]
    own_k.wait()
    arrive(to_k, ksem)
    ring_first(kbuf, ksem_r, K_HOPS)
    arrive(to_v, vsem)
    ring_first(vbuf, vsem_r, V_HOPS)
    own_q.wait()
    arrive(to_q, qsem)

    mrun[...] = jnp.full_like(mrun, NEG)
    lrun[...] = jnp.zeros_like(lrun)
    ot[...] = jnp.zeros_like(ot)
    dqt[...] = jnp.zeros_like(dqt)

    def forward(block, diagonal, heads=tuple(range(GROUP))):
        k = kbuf[block]
        ktbuf[block] = k.T
        v_t = jnp.concatenate([vbuf[block].T, jnp.ones((16, BLK), BF)], axis=0)
        if diagonal:
            allowed = lax.broadcasted_iota(jnp.int32, (BLK, BLK), 0) <= lax.broadcasted_iota(
                jnp.int32, (BLK, BLK), 1
            )

        def weigh(h, s):
            if diagonal:
                s = jnp.where(allowed, s, NEG)
            m_old = mrun[h]
            m_new = jnp.maximum(m_old, jnp.max(s, axis=0, keepdims=True))
            shift = m_new * C2
            p = jnp.exp2(s * C2 - shift).astype(BF)
            pbuf[block * GROUP + h] = p
            mhist[block * GROUP + h] = m_new
            mrun[h] = m_new
            return p, jnp.exp2(m_old * C2 - shift)

        def gather(h, p, shrink):
            o = dot(v_t, p)
            ot[h] = ot[h] * shrink + o[:HEAD]
            lrun[h] = lrun[h] * shrink + o[HEAD:HEAD + 1]

        s = dot(k, qt[heads[0]])
        held = None
        for h in heads:
            s_next = dot(k, qt[h + 1]) if h < heads[-1] else None
            if held is not None:
                gather(*held)
            held = (h, *weigh(h, s))
            s = s_next
        gather(*held)

    def pass_on(buf, sems, hops, step):
        ups, dns, parts = hops
        for part in range(parts):
            first = part * (NZ - 1)

            @pl.when((z - step >= 0) & (step <= ups))
            def _():
                wait_recv(ring_at(buf, z - step, part, parts), sems, first + step - 1)
                pl.when(step < ups)(lambda: ring_send(buf, sems, hops, True, step + 1, part))

            @pl.when(((z + step) % NZ < dns) & (step <= dns))
            def _():
                wait_recv(ring_at(buf, z + step, part, parts), sems, first + ups + step - 1)
                pl.when(step < dns)(lambda: ring_send(buf, sems, hops, False, step + 1, part))

    early = Q_FIRST // HEAD
    for h in range(early):
        qt[h] = qbuf[:, h * HEAD:(h + 1) * HEAD].T
    forward(z, True, tuple(range(early)))
    pass_on(kbuf, ksem_r, K_HOPS, 1)
    arrive(to_q2, qsem, 3)
    sent += exchange(lambda dst: do_in.at[:, lanes(dst * QG, QG)], to_do, osem)
    sent += exchange(lambda dst: hid_t.at[dst], to_hid, hsem)
    own_hid = pltpu.make_async_copy(hid_t.at[x], to_hid(x), lsem.at[8])
    own_hid.start()
    for h in range(early, GROUP):
        qt[h] = qbuf[:, h * HEAD:(h + 1) * HEAD].T
    forward(z, True, tuple(range(early, GROUP)))
    pass_on(vbuf, vsem_r, V_HOPS, 1)

    def forward_step(step, carry):
        below = (z + step) % NZ
        pl.when(z - step >= 0)(lambda: forward((z - step + NZ) % NZ, False))
        pass_on(kbuf, ksem_r, K_HOPS, step + 1)
        pl.when((step < STEPS) & (below < NZ - 1 - STEPS) & (below < z))(lambda: forward(below, False))
        pass_on(vbuf, vsem_r, V_HOPS, step + 1)
        return carry

    lax.fori_loop(1, STEPS + 1, forward_step, 0)

    own_do.wait()
    arrive(to_do, osem)
    for h in range(GROUP):
        lrun[h] = 1.0 / lrun[h]

    def hop_copy(send, recv, sems, up, slot, part, parts):
        at = pl.ds(part * (BLK // parts), BLK // parts)
        return remote(
            send.at[slot, at], recv.at[slot, at], sems, part * (NZ - 1) + slot, at_z(1 if up else NZ - 1)
        )

    def hop_plan(hops, step, up):
        ups = hops[1]
        if up:
            block = (z + ups + 1 - step) % NZ
            return block, (step <= ups) & (block < ups), hops[0] + step - 1
        block = z - hops[0] - 1 + step
        return (block + NZ) % NZ, (step <= hops[0]) & (block >= 0), step - 1

    def reduce_step(step, term, send, recv, sems, plan):
        parts = len(plan)
        size = BLK // parts
        for part in range(parts):
            at = pl.ds(part * size, size)
            for up in (False, True):
                block, valid, slot = hop_plan(plan[part], step, up)

                @pl.when(valid)
                def _():
                    if up:

                        @pl.when(block < z)
                        def _():
                            acc[:size] = term(block, part, parts)

                        @pl.when(block >= z)
                        def _():
                            acc[:size] = jnp.zeros((size, HEAD), F32)
                    else:
                        acc[:size] = term(block, part, parts)

                    @pl.when((step >= 2) if up else (step >= 2) & (z < NZ - 1))
                    def _():
                        wait_recv(recv.at[slot - 1, at], sems, part * (NZ - 1) + slot - 1)
                        acc[:size] += recv[slot - 1, at].astype(F32)

                    send[slot, at] = acc[:size].astype(BF)
                    hop_copy(send, recv, sems, up, slot, part, parts).start()

    def reduce_last(term, target, recv, sems, plan, done=lambda part, at: None):
        parts = len(plan)
        size = BLK // parts
        for part, (dns, ups) in enumerate(plan):
            at = pl.ds(part * size, size)
            acc[:size] = term(z, part, parts)
            for valid, slot in ((z < NZ - 1, dns - 1), (z < ups, dns + ups - 1)):

                @pl.when(valid)
                def _():
                    wait_recv(recv.at[slot, at], sems, part * (NZ - 1) + slot)
                    acc[:size] += recv[slot, at].astype(F32)

            target[at] = acc[:size].astype(BF)
            done(part, at)

    def reduce_sent(send, recv, sems, plan):
        for part in range(len(plan)):
            for up in (False, True):
                for step in range(1, STEPS + 1):
                    if step <= plan[part][1 if up else 0]:
                        _, valid, slot = hop_plan(plan[part], step, up)
                        pl.when(valid)(
                            lambda: hop_copy(send, recv, sems, up, slot, part, len(plan)).wait_send()
                        )

    def value_term(block, part=0, parts=1):
        keys = pl.ds(part * (BLK // parts), BLK // parts)
        total = None
        for h in range(GROUP):
            at = block * GROUP + h
            factor = jnp.exp2((mhist[at] - mrun[h]) * C2) * lrun[h]
            p = (pbuf[at, keys].astype(F32) * factor).astype(BF)
            pbuf[at, keys] = p
            term = dot(p, dobuf[:, h * HEAD:(h + 1) * HEAD])
            total = term if total is None else total + term
        return total

    def key_term(block, part=0, parts=1):
        keys = pl.ds(part * (BLK // parts), BLK // parts)
        v = vbuf[block, keys]
        k_t = ktbuf[block, :, pl.ds(part * (BLK // parts), BLK // parts)]
        total = None
        dp_next = dot(v, dot_t[0])
        for h in range(GROUP):
            dp_t = dp_next
            dp_next = dot(v, dot_t[h + 1]) if h + 1 < GROUP else None
            ds = (pbuf[block * GROUP + h, keys].astype(F32) * (dp_t - delta[h])).astype(BF)
            dqt[h] += dot(k_t, ds)
            term = dot(ds, qbuf[:, h * HEAD:(h + 1) * HEAD])
            total = term if total is None else total + term
        return total * SCALE

    to_att = lambda src: att_out.at[:, lanes(src * QG, QG)]
    own_att = pltpu.make_async_copy(o_own.at[mine], to_att(x), lsem.at[9])

    def att_copies():
        return [
            remote(o_own.at[rows((x + d) % NX * TOK, TOK)], to_att(x), asem, d - 1, at_x(d))
            for d in range(1, NX)
        ]

    def stage_attended():
        for h in range(GROUP):
            part = slice(h * HEAD, (h + 1) * HEAD)
            dot_t[h] = dobuf[:, part].T
            o = (ot[h] * lrun[h]).astype(BF)
            o_own[:, part] = o.T
            delta[h] = jnp.sum(o.astype(F32) * dot_t[h].astype(F32), axis=0, keepdims=True)
        for copy in att_copies():
            copy.start()
        own_att.start()

    def value_step(step, carry):
        reduce_step(step, value_term, vs, vr, rvsem, VALUE_HOPS)
        pl.when(step == 1)(stage_attended)
        return carry

    lax.fori_loop(1, STEPS + 1, value_step, 0)
    sibling = (y * 2 + 1 - c, ctx)
    hid_half = hid_r.at[:, :, lanes(c * BLK, BLK)]
    hid_copy2 = remote(hid_half, hid_half, csem, 0, sibling)

    def share(part, d):
        at = pl.ds(part * (BLK // len(VALUE_HOPS)), BLK // len(VALUE_HOPS))
        slot = (part * 2 + x % 2) * 2 + c
        return pltpu.make_async_remote_copy(
            src_ref=dv_own.at[at],
            dst_ref=dv_all.at[c, at, lanes(x % 2 * HEAD, HEAD)],
            send_sem=gvsem.at[0, part * NX + d],
            recv_sem=gvsem.at[1, slot],
            device_id=(y * 2 + x // 2, z * NX + (x + d) % NX),
            device_id_type=pl.DeviceIdType.MESH,
        )

    def share_all(part, at):
        for d in range(1, NX):
            share(part, d).start()
        pl.when(x // 2 != c)(lambda: share(part, 0).start())

        @pl.when(x // 2 == c)
        def _():
            dv_all[c, at, lanes(x % 2 * HEAD, HEAD)] = dv_own[at]

    reduce_last(value_term, dv_own, vr, rvsem, VALUE_HOPS, share_all)
    to_dv = lambda src: dv_out.at[:, lanes(src * HEAD, HEAD)]
    sent += exchange(lambda dst: dv_own.at[rows(dst * TOK, TOK)], to_dv, gosem)
    dv_out[:, lanes(x * HEAD, HEAD)] = dv_own[mine, :]

    halves = (0, 1)

    def y_start(index):
        return index * YROWS - jnp.maximum(index - 2, 0) * (YROWS - YLESS)

    def by_size(index, act):
        pl.when(index < 2)(lambda: act(YROWS))
        pl.when(index >= 2)(lambda: act(YLESS))

    def y_copy(i, d, size):
        to = (y + d) % 4
        return remote(
            w_y.at[i, :, rows(y_start(to), size)],
            w_yr.at[i, d - 1, :, pl.ds(0, size)],
            ysem,
            i * 3 + d - 1,
            (to * 2 + c, ctx),
        )

    def stage_hidden():
        own_hid.wait()
        arrive(to_hid, hsem)
        hid_copy2.start()

    def stage_product():
        hid_copy2.wait_recv()
        for part in range(len(VALUE_HOPS)):
            at = pl.ds(part * (BLK // len(VALUE_HOPS)), BLK // len(VALUE_HOPS))
            for j in (0, 1):
                for core in (0, 1):

                    @pl.when((x != c * 2 + j) | (c != core))
                    def _():
                        wait_recv(dv_all.at[core, at, pl.ds(j * HEAD, HEAD)], gvsem, (part * 2 + j) * 2 + core)

        h_rows = hid_r[...].reshape(NZ * ROWS, 2 * BLK)
        total = dot(h_rows, dv_all[...].reshape(2 * BLK, 256)).astype(BF)
        for i in halves:
            w_y[i] = total[:, i * HEAD:(i + 1) * HEAD].reshape(NZ, ROWS, HEAD)
            for d in range(1, 4):
                by_size((y + d) % 4, lambda size: y_copy(i, d, size).start())

    def z_copy(i, d, size):
        at = pl.ds(0, size)
        return remote(
            w_z.at[i, (z + d) % NZ, at], w_zr.at[i, d - 1, at], zsem, i * (NZ - 1) + d - 1, at_z(d)
        )

    def stage_z(size):
        for i in halves:
            total = w_y[i, :, rows(y_start(y), size), :].astype(F32)
            for d in range(1, 4):
                wait_recv(w_yr.at[i, d - 1, :, pl.ds(0, size)], ysem, i * 3 + d - 1)
                total += w_yr[i, d - 1, :, :size].astype(F32)
            w_z[i, :, :size] = total.astype(BF)
            for d in range(1, NZ):
                z_copy(i, d, size).start()

    def f_copy(i, d, size):
        target = w_all.at[c * 2 + i, rows(y_start(y), size)]
        return remote(w_f.at[i, pl.ds(0, size)], target, fsem, i * (NDP - 1) + d - 1, at_dp(d))

    def stage_f(size):
        for i in halves:
            total = w_z[i, z, :size].astype(F32)
            for d in range(1, NZ):
                wait_recv(w_zr.at[i, d - 1, pl.ds(0, size)], zsem, i * (NZ - 1) + d - 1)
                total += w_zr[i, d - 1, :size].astype(F32)
            w_f[i, :size] = (total * (1.0 / math.sqrt(32768.0))).astype(BF)
            w_all[c * 2 + i, rows(y_start(y), size), :] = w_f[i, :size]
            for d in range(1, NDP):
                f_copy(i, d, size).start()

    def key_step(step, carry):
        reduce_step(step, key_term, ks, kr, rksem, KEY_HOPS)
        pl.when(step == 1)(stage_hidden)
        pl.when(step == 2)(stage_product)
        return carry

    lax.fori_loop(1, STEPS + 1, key_step, 0)
    last = key_term(z)
    for h in range(GROUP):
        dq_own[:, h * HEAD:(h + 1) * HEAD] = (dqt[h] * SCALE).astype(BF).T
    to_dq = lambda src: dq_out.at[:, lanes(src * QG, QG)]
    sent += exchange(lambda dst: dq_own.at[rows(dst * TOK, TOK)], to_dq, dqsem)
    own_dq = pltpu.make_async_copy(dq_own.at[mine], to_dq(x), lsem.at[0])
    own_dq.start()
    by_size(y, stage_z)
    reduce_last(lambda block, part, parts: last[part * (BLK // parts):(part + 1) * (BLK // parts)], dk_own, kr, rksem, KEY_HOPS)
    to_dk = lambda src: dk_out.at[:, lanes(src * HEAD, HEAD)]
    sent += exchange(lambda dst: dk_own.at[rows(dst * TOK, TOK)], to_dk, gksem)
    dk_out[:, lanes(x * HEAD, HEAD)] = dk_own[mine, :]
    by_size(y, stage_f)

    own_dq.wait()
    own_att.wait()
    arrive(to_att, asem)
    for copy in sent + att_copies():
        copy.wait_send()
    for buf, sems, hops in ((kbuf, ksem_r, K_HOPS), (vbuf, vsem_r, V_HOPS)):
        for up in (True, False):
            for step in range(1, hops[0 if up else 1] + 1):
                for part in range(hops[2]):
                    ring_send(buf, sems, hops, up, step, part, lambda copy: copy.wait_send())
    reduce_sent(vs, vr, rvsem, VALUE_HOPS)
    reduce_sent(ks, kr, rksem, KEY_HOPS)
    for i in halves:
        for d in range(1, 4):
            by_size((y + d) % 4, lambda size: y_copy(i, d, size).wait_send())
        for d in range(1, NZ):
            by_size(y, lambda size: z_copy(i, d, size).wait_send())
    hid_copy2.wait_send()
    for part in range(len(VALUE_HOPS)):
        for d in range(1, NX):
            share(part, d).wait_send()
        pl.when(x // 2 != c)(lambda: share(part, 0).wait_send())
    arrive(to_dv, gosem)
    arrive(to_dk, gksem)
    arrive(to_dq, dqsem)
    for i in halves:
        for d in range(1, NDP):
            src = (dp + NDP - d) % NDP

            def done(size):
                target = w_all.at[src % 2 * 2 + i, rows(y_start(src // 2), size)]
                wait_recv(target, fsem, i * (NDP - 1) + d - 1)

            by_size(src // 2, done)
            by_size(y, lambda size: f_copy(i, d, size).wait_send())


def finish(att, dq, dk, dv, w, att_out, dq_out, dk_out, dv_out, w_out):
    att_out[...] = att[...]
    dq_out[...] = dq[...].astype(F32)
    dk_out[...] = dk[...].astype(F32)
    dv_out[...] = dv[...].astype(F32)
    for i in range(4):
        w_out[:, i * HEAD:(i + 1) * HEAD] = w[i].astype(F32)


def per_device(hidden_in, value_weight, queries, keys, out_grad):
    vmem = pl.BlockSpec(memory_space=pltpu.VMEM)
    anywhere = pl.BlockSpec(memory_space=pl.ANY)
    dma = pltpu.SemaphoreType.DMA
    parts = pl.pallas_call(
        kernel,
        out_shape=[
            jax.ShapeDtypeStruct((TOK, 2560), BF),
            jax.ShapeDtypeStruct((TOK, 2560), BF),
            jax.ShapeDtypeStruct((TOK, 512), BF),
            jax.ShapeDtypeStruct((TOK, 512), BF),
            jax.ShapeDtypeStruct((4, ROWS, HEAD), BF),
        ],
        in_specs=[anywhere] * 5,
        out_specs=[anywhere, anywhere, vmem, vmem, vmem],
        scratch_shapes=[
            pltpu.VMEM((TOK, WIDTH), BF),
            pltpu.VMEM((WIDTH, 512), BF),
            pltpu.VMEM((TOK, 512), BF),
            pltpu.VMEM((BLK, QG), BF),
            pltpu.VMEM((BLK, QG), BF),
            pltpu.VMEM((NZ, BLK, HEAD), BF),
            pltpu.VMEM((NZ, BLK, HEAD), BF),
            pltpu.VMEM((NZ, HEAD, BLK), BF),
            pltpu.VMEM((GROUP, HEAD, BLK), BF),
            pltpu.VMEM((GROUP, HEAD, BLK), BF),
            pltpu.VMEM((NZ * GROUP, BLK, BLK), BF),
            pltpu.VMEM((NZ * GROUP, 1, BLK), F32),
            pltpu.VMEM((GROUP, 1, BLK), F32),
            pltpu.VMEM((GROUP, 1, BLK), F32),
            pltpu.VMEM((GROUP, 1, BLK), F32),
            pltpu.VMEM((GROUP, HEAD, BLK), F32),
            pltpu.VMEM((GROUP, HEAD, BLK), F32),
            pltpu.VMEM((BLK, QG), BF),
            pltpu.VMEM((BLK, QG), BF),
            pltpu.VMEM((NX, NZ, ROWS, TOK), BF),
            pltpu.VMEM((NZ, ROWS, 2 * BLK), BF),
            pltpu.VMEM((BLK, HEAD), F32),
            pltpu.VMEM((NZ - 1, BLK, HEAD), BF),
            pltpu.VMEM((NZ - 1, BLK, HEAD), BF),
            pltpu.VMEM((NZ - 1, BLK, HEAD), BF),
            pltpu.VMEM((NZ - 1, BLK, HEAD), BF),
            pltpu.VMEM((BLK, HEAD), BF),
            pltpu.VMEM((BLK, HEAD), BF),
            pltpu.VMEM((2, BLK, 256), BF),
            pltpu.VMEM((2, NZ, ROWS, HEAD), BF),
            pltpu.VMEM((2, 3, NZ, YROWS, HEAD), BF),
            pltpu.VMEM((2, NZ, YROWS, HEAD), BF),
            pltpu.VMEM((2, NZ - 1, YROWS, HEAD), BF),
            pltpu.VMEM((2, YROWS, HEAD), BF),
            dma((10,)),
            dma((2, 6)),
            dma((2, 3)),
            dma((2, 3)),
            dma((2, 3)),
            dma((2, 3)),
            dma((2, 3)),
            dma((2, 3)),
            dma((2, 16)),
            dma((2, 3)),
            dma((2, 3)),
            dma((2, NZ - 1)),
            dma((2, 2 * (NZ - 1))),
            dma((2, 4 * (NZ - 1))),
            dma((2, 2 * (NZ - 1))),
            dma((2, 1)),
            dma((2, 6)),
            dma((2, 2 * (NZ - 1))),
            dma((2, 2 * (NDP - 1))),
        ],
        compiler_params=pltpu.CompilerParams(
            collective_id=0, has_side_effects=True, vmem_limit_bytes=60 * 2**20
        ),
    )(hidden_in[0], value_weight, queries[0], keys[0], out_grad[0])
    att, dq, dk, dv, w = pl.pallas_call(
        finish,
        out_shape=[
            jax.ShapeDtypeStruct((TOK, 2560), BF),
            jax.ShapeDtypeStruct((TOK, 2560), F32),
            jax.ShapeDtypeStruct((TOK, 512), F32),
            jax.ShapeDtypeStruct((TOK, 512), F32),
            jax.ShapeDtypeStruct((ROWS, 512), F32),
        ],
        in_specs=[vmem] * 5,
        out_specs=[vmem] * 5,
    )(*parts)
    return (att[None], dq[None], dk[None], dv[None], w)


def solution(mesh):
    return jax.shard_map(
        per_device,
        mesh=mesh,
        in_specs=(
            P("dp", "ctx", None),
            P(),
            P("dp", "ctx", None),
            P("dp", "ctx", None),
            P("dp", "ctx", None),
        ),
        out_specs=(
            P("dp", "ctx", None),
            P("dp", "ctx", None),
            P("dp", "ctx", None),
            P("dp", "ctx", None),
            P("ctx", None),
        ),
        check_vma=False,
    )
```
